32 devices in a mesh: expert: 32 (over z, y, x, core).
Axes of the slice: x: 2, y: 2, z: 4, core: 2. Of those that a mesh axis runs over, the one named last changes fastest.
Arguments:
- tokens: bfloat16 [4096, 4096], P('expert'), may hold values from -6 to 6
- norm_gain: float32 [4096], replicated, may hold values from 0.5 to 1.5
- router_weight: bfloat16 [4096, 32], replicated, may hold values from -0.09375 to 0.09375
- expert_ids: int32 [4096, 2], P('expert'), may hold values from 0 to 31, as said below
- gate_proj: bfloat16 [32, 4096, 768], P('expert'), may hold values from -0.09375 to 0.09375
- up_proj: bfloat16 [32, 4096, 768], P('expert'), may hold values from -0.09375 to 0.09375
- down_proj: bfloat16 [32, 768, 4096], P('expert'), may hold values from -0.21875 to 0.21875
- value_weight: bfloat16 [4096], replicated, may hold values from -0.09375 to 0.09375
- value_target: int32 [4096], P('expert'), may hold values from -1 to 1
- recency: float32 [4096], P('expert'), may hold values from 0.25 to 18, as said below
Outputs:
- mixed: bfloat16 [4096, 4096], P('expert')
- values: float32 [4096], P('expert')
- loss: float32 [], replicated
The draws below stay inside these ranges and needn't reach their ends.
Inputs may be any that keep to these rules, and one draw needn't show every extreme that they name: `expert_ids`: each row names two different experts; among the rows of one device no expert is named more than 12 times. `recency`: positive weights.
All inputs are finite; a program needn't handle non-finite values.
Results may differ from the reference program's by a relative error of at most 0.0055.
Values may be sent and summed in bfloat16 or wider, within the bound.
A program may use at most 128 MiB of HBM per device.

```python
import jax
import jax.numpy as jnp
from jax import lax

D = 4096
FF = 768
TOK_DEV = 128
EXPERTS = 32
CAP = 12
TOKENS = 4096
N_EXPERT = 32


def draw_expert_ids(key, part):
    key_hot, key_blocks = jax.random.split(jax.random.fold_in(key, 11))
    hottest = jax.random.randint(key_hot, (), 0, EXPERTS)
    block_keys = jax.random.split(key_blocks, TOKENS // TOK_DEV)
    base = jnp.repeat(jnp.arange(EXPERTS - 1, dtype=jnp.int32), CAP, total_repeat_length=(EXPERTS - 1) * CAP)
    others = base + (base >= hottest).astype(jnp.int32)

    def one_block(block_key):
        key_pool, key_rows, key_flip = jax.random.split(block_key, 3)
        shuffled = jax.random.permutation(key_pool, others)
        chosen = shuffled[:2 * TOK_DEV - CAP]
        everything = jnp.concatenate([jnp.full((CAP,), hottest, dtype=jnp.int32), chosen])
        ordered = jnp.sort(everything)
        paired = jnp.stack([ordered[:TOK_DEV], ordered[TOK_DEV:]], axis=1)
        paired = paired[jax.random.permutation(key_rows, TOK_DEV)]
        flipped = jax.random.randint(key_flip, (TOK_DEV, 1), 0, 2)
        return jnp.where(flipped == 1, paired[:, ::-1], paired)
    return lax.map(one_block, block_keys).reshape(TOKENS, 2).astype(jnp.int32)


def draw_recency(key, part):
    position = jnp.arange(TOKENS, dtype=jnp.float32) / TOKENS
    trend = jnp.exp(jnp.log(3.0) * position)
    noise_key = jax.random.fold_in(key, 23)
    noise = jax.random.uniform(noise_key, (TOKENS,), jnp.float32, 0.5, 1.5)
    return (trend * noise).astype(jnp.float32)


def set_ends(entries, key, least, largest):
    index_at = [jax.random.randint(jax.random.fold_in(key, axis), (), 0, length) for axis, length in enumerate(entries.shape)]
    longest = entries.shape.index(max(entries.shape))
    next_to = index_at[:longest] + [(index_at[longest] + 1) % entries.shape[longest]] + index_at[longest + 1:]
    return entries.at[tuple(index_at)].set(least).at[tuple(next_to)].set(largest)


def levels(key, dims, cuts, least, high):
    factor_of, own = 1.0, jax.random.fold_in(key, 6)
    for dim, parts in cuts:
        steps = jnp.exp(jax.random.uniform(jax.random.fold_in(own, dim), (parts,), jnp.float32, least / len(cuts), high / len(cuts)))
        factor_of = factor_of * jnp.repeat(steps, dims[dim] // parts).reshape([-1 if axis == dim else 1 for axis in range(len(dims))])
    return factor_of


def scatter_about(rng, extent, width, most, cuts=(), held_as=jnp.bfloat16):
    array = jax.random.normal(rng, extent, jnp.float32) * width
    if len(cuts) > 0:
        array = levels(rng, extent, cuts, -0.22, 0.18) * array
    return jnp.clip(array, min=-most, max=most).astype(held_as)


def setup_inputs(seed: int = 0) -> dict:
    seeds = jax.random.split(jax.random.key(seed), 11)
    tokens = scatter_about(seeds[0], (TOKENS, D), 1.0, 6.0, ((0, 32),))
    norm_gain = jnp.clip(1.0 + 0.1 * jax.random.normal(seeds[1], (D,), jnp.float32), 0.5, 1.5)
    router_weight = scatter_about(seeds[2], (D, EXPERTS), D ** -0.5, 0.09375)
    expert_ids = draw_expert_ids(jax.random.fold_in(seeds[10], 71), 0)
    gate_proj = scatter_about(seeds[4], (EXPERTS, D, FF), D ** -0.5, 0.09375, ((0, 32),))
    up_proj = scatter_about(seeds[5], (EXPERTS, D, FF), D ** -0.5, 0.09375, ((0, 32),))
    down_proj = scatter_about(seeds[6], (EXPERTS, FF, D), FF ** -0.5, 0.21875, ((0, 32),))
    value_weight = scatter_about(seeds[7], (D,), D ** -0.5, 0.09375)
    value_target = set_ends(jax.random.randint(seeds[8], (TOKENS,), -1, 2), jax.random.fold_in(seeds[8], 1), -1, 1).astype(jnp.int32)
    recency = draw_recency(jax.random.fold_in(seeds[10], 71), 0)
    return dict(tokens=tokens, norm_gain=norm_gain, router_weight=router_weight, expert_ids=expert_ids, gate_proj=gate_proj, up_proj=up_proj, down_proj=down_proj, value_weight=value_weight, value_target=value_target, recency=recency)


def block_ranks(flat_ids):
    columns = jnp.arange(EXPERTS, dtype=jnp.int32)
    one_hot = (flat_ids[:, None] == columns[None, :]).astype(jnp.int32)
    return lax.optimization_barrier(jnp.sum(jnp.cumsum(one_hot, axis=0) * one_hot, axis=1)) - 1

def reference(tokens, norm_gain, router_weight, expert_ids, gate_proj, up_proj, down_proj, value_weight, value_target, recency):
    wide = tokens.astype(jnp.float32)
    inverse = lax.rsqrt(lax.optimization_barrier(jnp.mean(wide * wide, axis=1, keepdims=True)) + 1e-05)
    normed = (wide * inverse * norm_gain).astype(jnp.bfloat16)
    logits = jnp.dot(normed, router_weight, preferred_element_type=jnp.float32)
    columns = jnp.arange(EXPERTS, dtype=jnp.int32)[None, :]
    first = lax.optimization_barrier(jnp.sum(jnp.where(expert_ids[:, 0:1] == columns, logits, 0.0), axis=1))
    second = lax.optimization_barrier(jnp.sum(jnp.where(expert_ids[:, 1:2] == columns, logits, 0.0), axis=1))
    gate_first = jax.nn.sigmoid(first - second)
    gate_second = jax.nn.sigmoid(second - first)
    grouped = expert_ids.reshape(N_EXPERT, 2 * TOK_DEV)
    ranks = jax.vmap(block_ranks)(grouped)
    per_expert = N_EXPERT * CAP
    block_index = jnp.arange(N_EXPERT, dtype=jnp.int32)[:, None]
    slot_global = (grouped * per_expert + block_index * CAP + ranks).reshape(-1).astype(jnp.int32)
    row_index = (jnp.arange(2 * TOKENS, dtype=jnp.int32) // 2).astype(jnp.int32)
    table = jnp.full((EXPERTS * per_expert,), TOKENS, dtype=jnp.int32).at[slot_global].set(row_index)
    padded = jnp.concatenate([normed, jnp.zeros((1, D), jnp.bfloat16)], axis=0)

    def one_expert(operands):
        indices, gate_mat, up_mat, down_mat = operands
        gathered = padded[indices]
        gate_part = jnp.dot(gathered, gate_mat, preferred_element_type=jnp.float32)
        up_part = jnp.dot(gathered, up_mat, preferred_element_type=jnp.float32)
        hidden = (jax.nn.silu(gate_part) * up_part).astype(jnp.bfloat16)
        return jnp.dot(hidden, down_mat, preferred_element_type=jnp.float32).astype(jnp.bfloat16)
    produced = lax.map(one_expert, (table.reshape(EXPERTS, per_expert), gate_proj, up_proj, down_proj))
    flat_out = produced.reshape(EXPERTS * per_expert, D)
    picked = flat_out[slot_global].reshape(TOKENS, 2, D)
    mixed = (wide + gate_first[:, None] * picked[:, 0].astype(jnp.float32) + gate_second[:, None] * picked[:, 1].astype(jnp.float32)).astype(jnp.bfloat16)
    values = jnp.tanh(jnp.dot(mixed, value_weight, preferred_element_type=jnp.float32))
    error = values - value_target.astype(jnp.float32)
    loss = jnp.sum(recency * error * error) / jnp.sum(recency)
    return (mixed, values, loss)
```

```python
import functools

import jax
import jax.numpy as jnp
import numpy as np
from jax import lax
from jax.experimental import pallas as pl
from jax.experimental.pallas import tpu as pltpu
from jax.sharding import PartitionSpec as P

BLOCKS = 4
MESH = pl.DeviceIdType.MESH
F32 = jnp.float32
BF16 = jnp.bfloat16


def to_column(row):
    t = row.shape[1]
    shape = (t, t)
    eye = lax.broadcasted_iota(jnp.int32, shape, 0) == lax.broadcasted_iota(jnp.int32, shape, 1)
    return jnp.sum(jnp.where(eye, row, 0.0), axis=1, keepdims=True)


def to_row(column):
    t = column.shape[0]
    shape = (t, t)
    eye = lax.broadcasted_iota(jnp.int32, shape, 0) == lax.broadcasted_iota(jnp.int32, shape, 1)
    return jnp.sum(jnp.where(eye, column, 0.0), axis=0, keepdims=True)


def kernel(
    axis, n, cap, parts,
    tok_ref, gain_ref, router_ref, ids_ref, head_ref, target_ref, recency_ref, split_ref, merge_ref,
    gate_hbm, up_hbm, down_hbm,
    mixed_ref, values_ref, loss_ref,
    gate_v, up_v, down_v, normed, send, recv, xs, ys, yout, ret, acc, sums, all_sums,
    w_sem, s1, r1, s2, r2, s3, r3,
):
    tokens, width = tok_ref.shape
    part = width // parts
    per = n // BLOCKS
    rows = per * cap * parts
    flat = per * cap
    me = lax.axis_index(axis)
    mine, place = me // per, lax.rem(me, per)

    def block_of(h):
        high = lax.rem(mine // 2 + h // 2, 2)
        low = lax.rem(lax.rem(mine, 2) + lax.rem(h, 2), 2)
        return 2 * high + low

    weights = [
        pltpu.make_async_copy(gate_hbm.at[0], gate_v, w_sem.at[0]),
        pltpu.make_async_copy(up_hbm.at[0], up_v, w_sem.at[1]),
        pltpu.make_async_copy(down_hbm.at[0], down_v, w_sem.at[2]),
    ]
    barrier = pltpu.get_barrier_semaphore()

    def greet(s, _):
        pl.semaphore_signal(barrier, inc=1, device_id=(lax.rem(me + s, n),), device_id_type=MESH)
        return 0

    lax.fori_loop(1, n, greet, 0)
    for copy in weights:
        copy.start()

    experts = lax.broadcasted_iota(jnp.int32, (n, tokens), 0)
    hot0 = (experts == ids_ref[0:1, :]).astype(F32)
    hot1 = (experts == ids_ref[1:2, :]).astype(F32)
    square = (tokens, tokens)
    before = (
        lax.broadcasted_iota(jnp.int32, square, 0) < lax.broadcasted_iota(jnp.int32, square, 1)
    ).astype(F32).astype(BF16)
    earlier0 = jnp.dot(hot0.astype(BF16), before, preferred_element_type=F32)
    earlier1 = jnp.dot(hot1.astype(BF16), before, preferred_element_type=F32)
    count0 = jnp.sum(hot0, axis=1, keepdims=True)
    stride = float(cap * parts)
    base0 = jnp.sum(hot0 * earlier0, axis=0, keepdims=True) + ids_ref[0:1, :].astype(F32) * stride
    base1 = (
        jnp.sum(hot1 * (earlier1 + count0), axis=0, keepdims=True)
        + ids_ref[1:2, :].astype(F32) * stride
    )

    total = jnp.zeros((tokens, 1), F32)
    for q in range(parts):
        wide = tok_ref[:, q * part:(q + 1) * part].astype(F32)
        total += jnp.sum(wide * wide, axis=1, keepdims=True)
    inverse = lax.rsqrt(total / width + 1e-05)
    for q in range(parts):
        cut = slice(q * part, (q + 1) * part)
        normed[:, cut] = (tok_ref[:, cut].astype(F32) * inverse * gain_ref[:, cut]).astype(BF16)

    pl.semaphore_wait(barrier, n - 1)

    def out_copy(h, j):
        return pltpu.make_async_remote_copy(
            src_ref=send.at[h, j], dst_ref=recv.at[h, place],
            send_sem=s1.at[h, j], recv_sem=r1.at[h, place],
            device_id=(block_of(h) * per + j,), device_id_type=MESH,
        )

    def in_copy(h, j):
        return pltpu.make_async_remote_copy(
            src_ref=send.at[h, j], dst_ref=recv.at[h, j],
            send_sem=s1.at[h, j], recv_sem=r1.at[h, j],
            device_id=(block_of(h) * per + j,), device_id_type=MESH,
        )

    def back_copy(h, j):
        return pltpu.make_async_remote_copy(
            src_ref=yout.at[h, j], dst_ref=ret.at[h, place],
            send_sem=s2.at[h, j], recv_sem=r2.at[h, place],
            device_id=(block_of(h) * per + j,), device_id_type=MESH,
        )

    def home_copy(h, j):
        return pltpu.make_async_remote_copy(
            src_ref=yout.at[h, j], dst_ref=ret.at[h, j],
            send_sem=s2.at[h, j], recv_sem=r2.at[h, j],
            device_id=(block_of(h) * per + j,), device_id_type=MESH,
        )

    def each(h, act):
        def step(j, _):
            @pl.when(jnp.logical_or(h != 0, j != place))
            def _():
                act(j)
            return 0
        lax.fori_loop(0, per, step, 0)

    def dispatch(i, _):
        h = BLOCKS - 1 - i
        first = (block_of(h) * rows).astype(F32)
        at = lax.broadcasted_iota(jnp.int32, (rows, tokens), 0).astype(F32) + first
        picked = jnp.zeros((rows, part), F32)
        for q in range(parts):
            shift = float(q * cap)
            hot = jnp.logical_or(at == base0 + shift, at == base1 + shift)
            picked += jnp.dot(
                hot.astype(F32).astype(BF16), normed[:, q * part:(q + 1) * part],
                preferred_element_type=F32,
            )
        send[h] = picked.astype(BF16).reshape(per, cap * parts, part)
        each(h, lambda j: out_copy(h, j).start())
        return 0

    lax.fori_loop(0, BLOCKS, dispatch, 0)
    recv[0, place] = send[0, place]

    logits = lax.dot_general(
        router_ref[...], normed[...], (((1,), (1,)), ((), ())), preferred_element_type=F32
    )
    first = jnp.sum(hot0 * logits, axis=0, keepdims=True)
    second = jnp.sum(hot1 * logits, axis=0, keepdims=True)
    weight0 = to_column(jax.nn.sigmoid(first - second))
    weight1 = to_column(jax.nn.sigmoid(second - first))
    column0, column1 = to_column(base0), to_column(base1)
    acc[...] = tok_ref[...].astype(F32)
    for copy in weights:
        copy.wait()

    def ffn(i, _):
        h = BLOCKS - 1 - i
        each(h, lambda j: in_copy(h, j).wait_recv())
        xs[...] = jnp.dot(
            split_ref[...], recv[h].reshape(rows, part), preferred_element_type=F32
        ).astype(BF16)
        hidden = gate_v.shape[1]
        gate = jnp.zeros((flat, hidden), F32)
        up = jnp.zeros((flat, hidden), F32)
        for q in range(parts):
            x = xs[q * flat:(q + 1) * flat, :]
            gate += jnp.dot(x, gate_v[q * part:(q + 1) * part, :], preferred_element_type=F32)
            up += jnp.dot(x, up_v[q * part:(q + 1) * part, :], preferred_element_type=F32)
        act = (gate / (1.0 + jnp.exp(-gate)) * up).astype(BF16)
        for q in range(parts):
            ys[q * flat:(q + 1) * flat, :] = jnp.dot(
                act, down_v[:, q * part:(q + 1) * part], preferred_element_type=F32
            ).astype(BF16)
        yout[h] = jnp.dot(
            merge_ref[...], ys[...], preferred_element_type=F32
        ).astype(BF16).reshape(per, cap * parts, part)
        each(h, lambda j: back_copy(h, j).start())
        return 0

    lax.fori_loop(0, BLOCKS, ffn, 0)
    ret[0, place] = yout[0, place]

    def combine(h, _):
        each(h, lambda j: home_copy(h, j).wait_recv())
        start = (block_of(h) * rows).astype(F32)
        at = lax.broadcasted_iota(jnp.int32, (tokens, rows), 1).astype(F32) + start
        back = ret[h].reshape(rows, part)
        for q in range(parts):
            shift = float(q * cap)
            cut = slice(q * part, (q + 1) * part)
            hot_a = (at == column0 + shift).astype(F32).astype(BF16)
            hot_b = (at == column1 + shift).astype(F32).astype(BF16)
            acc[:, cut] += weight0 * jnp.dot(hot_a, back, preferred_element_type=F32)
            acc[:, cut] += weight1 * jnp.dot(hot_b, back, preferred_element_type=F32)
        return 0

    lax.fori_loop(0, BLOCKS, combine, 0)

    score = jnp.zeros((tokens, 1), F32)
    for q in range(parts):
        cut = slice(q * part, (q + 1) * part)
        mixed = acc[:, cut].astype(BF16)
        mixed_ref[:, cut] = mixed
        score += jnp.sum(
            mixed.astype(F32) * head_ref[:, cut].astype(F32), axis=1, keepdims=True
        )
    values = jnp.tanh(to_row(score))
    values_ref[...] = values
    error = values - target_ref[...].astype(F32)
    recency = recency_ref[...]
    weighted = jnp.sum(recency * error * error, axis=1, keepdims=True)
    weight = jnp.sum(recency, axis=1, keepdims=True)
    lane = lax.broadcasted_iota(jnp.int32, sums.shape, 1)
    sums[...] = jnp.where(lane == 0, weighted, jnp.where(lane == 1, weight, 0.0))
    all_sums[me] = sums[...]

    def sum_copy(to, slot):
        return pltpu.make_async_remote_copy(
            src_ref=sums, dst_ref=all_sums.at[slot],
            send_sem=s3.at[to], recv_sem=r3.at[slot],
            device_id=(to,), device_id_type=MESH,
        )

    def share(s, _):
        sum_copy(lax.rem(me + s, n), me).start()
        return 0

    lax.fori_loop(1, n, share, 0)

    def drain(h, _):
        each(h, lambda j: out_copy(h, j).wait_send())
        each(h, lambda j: back_copy(h, j).wait_send())
        return 0

    lax.fori_loop(0, BLOCKS, drain, 0)

    def take(s, _):
        other = lax.rem(me + s, n)
        sum_copy(other, other).wait_recv()
        return 0

    lax.fori_loop(1, n, take, 0)
    whole = jnp.sum(all_sums[...], axis=0)
    loss_ref[...] = whole[0:1, 0:1] / whole[0:1, 1:2]

    def leave(s, _):
        other = lax.rem(me + s, n)
        sum_copy(other, other).wait_send()
        return 0

    lax.fori_loop(1, n, leave, 0)


def body(
    axis,
    n,
    tokens,
    norm_gain,
    router_weight,
    expert_ids,
    gate_proj,
    up_proj,
    down_proj,
    value_weight,
    value_target,
    recency,
):
    count, width = tokens.shape
    hidden = gate_proj.shape[2]
    cap = 3 * count // n
    parts = 1
    while cap * parts % 16:
        parts *= 2
    part = width // parts
    per = n // BLOCKS
    rows, flat = per * cap * parts, per * cap
    order = np.arange(rows).reshape(per, parts, cap).transpose(1, 0, 2).reshape(-1)
    split = np.zeros((rows, rows), np.float32)
    split[np.arange(rows), order] = 1.0
    merge = jnp.asarray(split.T, BF16)
    split = jnp.asarray(split, BF16)
    vmem = pl.BlockSpec(memory_space=pltpu.VMEM)
    block = (BLOCKS, per, cap * parts, part)
    dma = pltpu.SemaphoreType.DMA
    mixed, values, loss = pl.pallas_call(
        functools.partial(kernel, axis, n, cap, parts),
        out_shape=(
            jax.ShapeDtypeStruct((count, width), BF16),
            jax.ShapeDtypeStruct((1, count), F32),
            jax.ShapeDtypeStruct((1, 1), F32),
        ),
        in_specs=[vmem] * 9 + [pl.BlockSpec(memory_space=pl.ANY)] * 3,
        out_specs=(vmem, vmem, vmem),
        scratch_shapes=[
            pltpu.VMEM((width, hidden), BF16),
            pltpu.VMEM((width, hidden), BF16),
            pltpu.VMEM((hidden, width), BF16),
            pltpu.VMEM((count, width), BF16),
            pltpu.VMEM(block, BF16),
            pltpu.VMEM(block, BF16),
            pltpu.VMEM((rows, part), BF16),
            pltpu.VMEM((rows, part), BF16),
            pltpu.VMEM(block, BF16),
            pltpu.VMEM(block, BF16),
            pltpu.VMEM((count, width), F32),
            pltpu.VMEM((8, 128), F32),
            pltpu.VMEM((n, 8, 128), F32),
            dma((3,)),
            dma((BLOCKS, per)),
            dma((BLOCKS, per)),
            dma((BLOCKS, per)),
            dma((BLOCKS, per)),
            dma((n,)),
            dma((n,)),
        ],
        compiler_params=pltpu.CompilerParams(
            collective_id=0, has_side_effects=True, vmem_limit_bytes=60 * 2**20
        ),
        cost_estimate=pl.CostEstimate(
            flops=6 * n * cap * width * hidden,
            bytes_accessed=6 * width * hidden,
            transcendentals=n * cap * hidden,
        ),
    )(
        tokens,
        norm_gain.reshape(1, width),
        router_weight.T,
        expert_ids.T,
        value_weight.reshape(1, width),
        value_target.reshape(1, count),
        recency.reshape(1, count),
        split,
        merge,
        gate_proj,
        up_proj,
        down_proj,
    )
    return (mixed, values.reshape(count), loss.reshape(()))


def solution(mesh):
    axis = mesh.axis_names[0]
    return jax.shard_map(
        functools.partial(body, axis, mesh.shape[axis]),
        mesh=mesh,
        in_specs=(
            P(axis, None),
            P(),
            P(),
            P(axis, None),
            P(axis, None, None),
            P(axis, None, None),
            P(axis, None, None),
            P(),
            P(axis),
            P(axis),
        ),
        out_specs=(P(axis, None), P(axis), P()),
        check_vma=False,
    )
```

```python
import functools

import jax
import jax.numpy as jnp
import numpy as np
from jax import lax
from jax.experimental import pallas as pl
from jax.experimental.pallas import tpu as pltpu
from jax.sharding import PartitionSpec as P

BLOCKS = 4
SENT = (2, 3, 1, 0)
WORKED = (2, 3, 1, 0)
TAKEN = (2, 0, 1, 3)
MESH = pl.DeviceIdType.MESH
F32 = jnp.float32
BF16 = jnp.bfloat16


def to_column(row):
    t = row.shape[1]
    shape = (t, t)
    eye = lax.broadcasted_iota(jnp.int32, shape, 0) == lax.broadcasted_iota(jnp.int32, shape, 1)
    return jnp.sum(jnp.where(eye, row, 0.0), axis=1, keepdims=True)


def to_row(column):
    t = column.shape[0]
    shape = (t, t)
    eye = lax.broadcasted_iota(jnp.int32, shape, 0) == lax.broadcasted_iota(jnp.int32, shape, 1)
    return jnp.sum(jnp.where(eye, column, 0.0), axis=0, keepdims=True)


def kernel(
    axis, n, cap, parts,
    tok_ref, gain_ref, router_ref, ids_ref, head_ref, target_ref, recency_ref, split_ref, merge_ref,
    gate_hbm, up_hbm, down_hbm,
    mixed_ref, values_ref, loss_ref,
    gate_v, up_v, down_v, normed, send, recv, xs, ys, yout, ret, acc, sums, all_sums,
    w_sem, s1, r1, s2, r2, s3, r3,
):
    tokens, width = tok_ref.shape
    part = width // parts
    per = n // BLOCKS
    rows = per * cap * parts
    flat = per * cap
    me = lax.axis_index(axis)
    mine, place = me // per, lax.rem(me, per)

    def block_of(h):
        high = lax.rem(mine // 2 + h // 2, 2)
        low = lax.rem(lax.rem(mine, 2) + lax.rem(h, 2), 2)
        return 2 * high + low

    weights = [
        pltpu.make_async_copy(gate_hbm.at[0], gate_v, w_sem.at[0]),
        pltpu.make_async_copy(up_hbm.at[0], up_v, w_sem.at[1]),
        pltpu.make_async_copy(down_hbm.at[0], down_v, w_sem.at[2]),
    ]
    barrier = pltpu.get_barrier_semaphore()

    def greet(s, _):
        pl.semaphore_signal(barrier, inc=1, device_id=(lax.rem(me + s, n),), device_id_type=MESH)
        return 0

    lax.fori_loop(1, n, greet, 0)
    for copy in weights:
        copy.start()

    experts = lax.broadcasted_iota(jnp.int32, (n, tokens), 0)
    hot0 = (experts == ids_ref[0:1, :]).astype(F32)
    hot1 = (experts == ids_ref[1:2, :]).astype(F32)
    square = (tokens, tokens)
    before = (
        lax.broadcasted_iota(jnp.int32, square, 0) < lax.broadcasted_iota(jnp.int32, square, 1)
    ).astype(F32).astype(BF16)
    earlier0 = jnp.dot(hot0.astype(BF16), before, preferred_element_type=F32)
    earlier1 = jnp.dot(hot1.astype(BF16), before, preferred_element_type=F32)
    count0 = jnp.sum(hot0, axis=1, keepdims=True)
    stride = float(cap * parts)
    base0 = jnp.sum(hot0 * earlier0, axis=0, keepdims=True) + ids_ref[0:1, :].astype(F32) * stride
    base1 = (
        jnp.sum(hot1 * (earlier1 + count0), axis=0, keepdims=True)
        + ids_ref[1:2, :].astype(F32) * stride
    )

    total = jnp.zeros((tokens, 1), F32)
    for q in range(parts):
        wide = tok_ref[:, q * part:(q + 1) * part].astype(F32)
        total += jnp.sum(wide * wide, axis=1, keepdims=True)
    inverse = lax.rsqrt(total / width + 1e-05)
    for q in range(parts):
        cut = slice(q * part, (q + 1) * part)
        normed[:, cut] = (tok_ref[:, cut].astype(F32) * inverse * gain_ref[:, cut]).astype(BF16)

    pl.semaphore_wait(barrier, n - 1)

    def out_copy(h, j):
        return pltpu.make_async_remote_copy(
            src_ref=send.at[h, j], dst_ref=recv.at[h, place],
            send_sem=s1.at[h, j], recv_sem=r1.at[h, place],
            device_id=(block_of(h) * per + j,), device_id_type=MESH,
        )

    def in_copy(h, j):
        return pltpu.make_async_remote_copy(
            src_ref=send.at[h, j], dst_ref=recv.at[h, j],
            send_sem=s1.at[h, j], recv_sem=r1.at[h, j],
            device_id=(block_of(h) * per + j,), device_id_type=MESH,
        )

    def back_copy(h, j):
        return pltpu.make_async_remote_copy(
            src_ref=yout.at[h, j], dst_ref=ret.at[h, place],
            send_sem=s2.at[h, j], recv_sem=r2.at[h, place],
            device_id=(block_of(h) * per + j,), device_id_type=MESH,
        )

    def home_copy(h, j):
        return pltpu.make_async_remote_copy(
            src_ref=yout.at[h, j], dst_ref=ret.at[h, j],
            send_sem=s2.at[h, j], recv_sem=r2.at[h, j],
            device_id=(block_of(h) * per + j,), device_id_type=MESH,
        )

    def pick(order, i):
        return sum(jnp.where(i == k, h, 0) for k, h in enumerate(order))

    def each(h, act):
        def step(turn, _):
            j = lax.rem(place + turn, per)

            @pl.when(jnp.logical_or(h != 0, j != place))
            def _():
                act(j)
            return 0
        lax.fori_loop(0, per, step, 0)

    def dispatch(i, _):
        h = pick(SENT, i)
        first = (block_of(h) * rows).astype(F32)
        at = lax.broadcasted_iota(jnp.int32, (rows, tokens), 0).astype(F32) + first
        picked = jnp.zeros((rows, part), F32)
        for q in range(parts):
            shift = float(q * cap)
            hot = jnp.logical_or(at == base0 + shift, at == base1 + shift)
            picked += jnp.dot(
                hot.astype(F32).astype(BF16), normed[:, q * part:(q + 1) * part],
                preferred_element_type=F32,
            )
        send[h] = picked.astype(BF16).reshape(per, cap * parts, part)
        each(h, lambda j: out_copy(h, j).start())
        return 0

    lax.fori_loop(0, BLOCKS, dispatch, 0)
    recv[0, place] = send[0, place]

    logits = lax.dot_general(
        router_ref[...], normed[...], (((1,), (1,)), ((), ())), preferred_element_type=F32
    )
    first = jnp.sum(hot0 * logits, axis=0, keepdims=True)
    second = jnp.sum(hot1 * logits, axis=0, keepdims=True)
    weight0 = to_column(jax.nn.sigmoid(first - second))
    weight1 = to_column(jax.nn.sigmoid(second - first))
    column0, column1 = to_column(base0), to_column(base1)
    acc[...] = tok_ref[...].astype(F32)
    for copy in weights:
        copy.wait()

    def ffn(i, _):
        h = pick(WORKED, i)
        each(h, lambda j: in_copy(h, j).wait_recv())
        xs[...] = jnp.dot(
            split_ref[...], recv[h].reshape(rows, part), preferred_element_type=F32
        ).astype(BF16)
        hidden = gate_v.shape[1]
        gate = jnp.zeros((flat, hidden), F32)
        up = jnp.zeros((flat, hidden), F32)
        for q in range(parts):
            x = xs[q * flat:(q + 1) * flat, :]
            gate += jnp.dot(x, gate_v[q * part:(q + 1) * part, :], preferred_element_type=F32)
            up += jnp.dot(x, up_v[q * part:(q + 1) * part, :], preferred_element_type=F32)
        act = (gate / (1.0 + jnp.exp(-gate)) * up).astype(BF16)
        for q in range(parts):
            ys[q * flat:(q + 1) * flat, :] = jnp.dot(
                act, down_v[:, q * part:(q + 1) * part], preferred_element_type=F32
            ).astype(BF16)
        yout[h] = jnp.dot(
            merge_ref[...], ys[...], preferred_element_type=F32
        ).astype(BF16).reshape(per, cap * parts, part)
        each(h, lambda j: back_copy(h, j).start())
        return 0

    lax.fori_loop(0, BLOCKS, ffn, 0)
    ret[0, place] = yout[0, place]

    def combine(i, _):
        h = pick(TAKEN, i)
        each(h, lambda j: home_copy(h, j).wait_recv())
        start = (block_of(h) * rows).astype(F32)
        at = lax.broadcasted_iota(jnp.int32, (tokens, rows), 1).astype(F32) + start
        back = ret[h].reshape(rows, part)
        for q in range(parts):
            shift = float(q * cap)
            cut = slice(q * part, (q + 1) * part)
            hot_a = (at == column0 + shift).astype(F32).astype(BF16)
            hot_b = (at == column1 + shift).astype(F32).astype(BF16)
            acc[:, cut] += weight0 * jnp.dot(hot_a, back, preferred_element_type=F32)
            acc[:, cut] += weight1 * jnp.dot(hot_b, back, preferred_element_type=F32)
        return 0

    lax.fori_loop(0, BLOCKS, combine, 0)

    score = jnp.zeros((tokens, 1), F32)
    for q in range(parts):
        cut = slice(q * part, (q + 1) * part)
        mixed = acc[:, cut].astype(BF16)
        mixed_ref[:, cut] = mixed
        score += jnp.sum(
            mixed.astype(F32) * head_ref[:, cut].astype(F32), axis=1, keepdims=True
        )
    values = jnp.tanh(to_row(score))
    values_ref[...] = values
    error = values - target_ref[...].astype(F32)
    recency = recency_ref[...]
    weighted = jnp.sum(recency * error * error, axis=1, keepdims=True)
    weight = jnp.sum(recency, axis=1, keepdims=True)
    lane = lax.broadcasted_iota(jnp.int32, sums.shape, 1)
    sums[...] = jnp.where(lane == 0, weighted, jnp.where(lane == 1, weight, 0.0))
    all_sums[me] = sums[...]

    def sum_copy(to, slot):
        return pltpu.make_async_remote_copy(
            src_ref=sums, dst_ref=all_sums.at[slot],
            send_sem=s3.at[to], recv_sem=r3.at[slot],
            device_id=(to,), device_id_type=MESH,
        )

    def share(s, _):
        sum_copy(lax.rem(me + s, n), me).start()
        return 0

    lax.fori_loop(1, n, share, 0)

    def drain(h, _):
        each(h, lambda j: out_copy(h, j).wait_send())
        each(h, lambda j: back_copy(h, j).wait_send())
        return 0

    lax.fori_loop(0, BLOCKS, drain, 0)

    def take(s, _):
        other = lax.rem(me + s, n)
        sum_copy(other, other).wait_recv()
        return 0

    lax.fori_loop(1, n, take, 0)
    whole = jnp.sum(all_sums[...], axis=0)
    loss_ref[...] = whole[0:1, 0:1] / whole[0:1, 1:2]

    def leave(s, _):
        other = lax.rem(me + s, n)
        sum_copy(other, other).wait_send()
        return 0

    lax.fori_loop(1, n, leave, 0)


def body(
    axis,
    n,
    tokens,
    norm_gain,
    router_weight,
    expert_ids,
    gate_proj,
    up_proj,
    down_proj,
    value_weight,
    value_target,
    recency,
):
    count, width = tokens.shape
    hidden = gate_proj.shape[2]
    cap = 3 * count // n
    parts = 1
    while cap * parts % 16:
        parts *= 2
    part = width // parts
    per = n // BLOCKS
    rows, flat = per * cap * parts, per * cap
    order = np.arange(rows).reshape(per, parts, cap).transpose(1, 0, 2).reshape(-1)
    split = np.zeros((rows, rows), np.float32)
    split[np.arange(rows), order] = 1.0
    merge = jnp.asarray(split.T, BF16)
    split = jnp.asarray(split, BF16)
    vmem = pl.BlockSpec(memory_space=pltpu.VMEM)
    block = (BLOCKS, per, cap * parts, part)
    dma = pltpu.SemaphoreType.DMA
    mixed, values, loss = pl.pallas_call(
        functools.partial(kernel, axis, n, cap, parts),
        out_shape=(
            jax.ShapeDtypeStruct((count, width), BF16),
            jax.ShapeDtypeStruct((1, count), F32),
            jax.ShapeDtypeStruct((1, 1), F32),
        ),
        in_specs=[vmem] * 9 + [pl.BlockSpec(memory_space=pl.ANY)] * 3,
        out_specs=(vmem, vmem, vmem),
        scratch_shapes=[
            pltpu.VMEM((width, hidden), BF16),
            pltpu.VMEM((width, hidden), BF16),
            pltpu.VMEM((hidden, width), BF16),
            pltpu.VMEM((count, width), BF16),
            pltpu.VMEM(block, BF16),
            pltpu.VMEM(block, BF16),
            pltpu.VMEM((rows, part), BF16),
            pltpu.VMEM((rows, part), BF16),
            pltpu.VMEM(block, BF16),
            pltpu.VMEM(block, BF16),
            pltpu.VMEM((count, width), F32),
            pltpu.VMEM((8, 128), F32),
            pltpu.VMEM((n, 8, 128), F32),
            dma((3,)),
            dma((BLOCKS, per)),
            dma((BLOCKS, per)),
            dma((BLOCKS, per)),
            dma((BLOCKS, per)),
            dma((n,)),
            dma((n,)),
        ],
        compiler_params=pltpu.CompilerParams(
            collective_id=0, has_side_effects=True, vmem_limit_bytes=60 * 2**20
        ),
        cost_estimate=pl.CostEstimate(
            flops=6 * n * cap * width * hidden,
            bytes_accessed=6 * width * hidden,
            transcendentals=n * cap * hidden,
        ),
    )(
        tokens,
        norm_gain.reshape(1, width),
        router_weight.T,
        expert_ids.T,
        value_weight.reshape(1, width),
        value_target.reshape(1, count),
        recency.reshape(1, count),
        split,
        merge,
        gate_proj,
        up_proj,
        down_proj,
    )
    return (mixed, values.reshape(count), loss.reshape(()))


def solution(mesh):
    axis = mesh.axis_names[0]
    return jax.shard_map(
        functools.partial(body, axis, mesh.shape[axis]),
        mesh=mesh,
        in_specs=(
            P(axis, None),
            P(),
            P(),
            P(axis, None),
            P(axis, None, None),
            P(axis, None, None),
            P(axis, None, None),
            P(),
            P(axis),
            P(axis),
        ),
        out_specs=(P(axis, None), P(axis), P()),
        check_vma=False,
    )
```

```python
import functools

import jax
import jax.numpy as jnp
import numpy as np
from jax import lax
from jax.experimental import pallas as pl
from jax.experimental.pallas import tpu as pltpu
from jax.sharding import PartitionSpec as P

BLOCKS = 4
SENT = (2, 3, 1, 0)
WORKED = (2, 3, 1, 0)
TAKEN = (2, 0, 1, 3)
MESH = pl.DeviceIdType.MESH
F32 = jnp.float32
BF16 = jnp.bfloat16


def to_column(row):
    t = row.shape[1]
    shape = (t, t)
    eye = lax.broadcasted_iota(jnp.int32, shape, 0) == lax.broadcasted_iota(jnp.int32, shape, 1)
    return jnp.sum(jnp.where(eye, row, 0.0), axis=1, keepdims=True)


def to_row(column):
    t = column.shape[0]
    shape = (t, t)
    eye = lax.broadcasted_iota(jnp.int32, shape, 0) == lax.broadcasted_iota(jnp.int32, shape, 1)
    return jnp.sum(jnp.where(eye, column, 0.0), axis=0, keepdims=True)


def kernel(
    axis, n, cap, parts,
    tok_ref, gain_ref, router_ref, ids_ref, head_ref, target_ref, recency_ref, split_ref, merge_ref,
    gate_hbm, up_hbm, down_hbm,
    mixed_ref, values_ref, loss_ref,
    gate_v, up_v, down_v, normed, send, recv, xs, ys, yout, ret, acc, sums, all_sums,
    w_sem, s1, r1, s2, r2, s3, r3,
):
    tokens, width = tok_ref.shape
    part = width // parts
    per = n // BLOCKS
    rows = per * cap * parts
    flat = per * cap
    me = lax.axis_index(axis)
    mine, place = me // per, lax.rem(me, per)

    def block_of(h):
        high = lax.rem(mine // 2 + h // 2, 2)
        low = lax.rem(lax.rem(mine, 2) + lax.rem(h, 2), 2)
        return 2 * high + low

    weights = [
        pltpu.make_async_copy(gate_hbm.at[0], gate_v, w_sem.at[0]),
        pltpu.make_async_copy(up_hbm.at[0], up_v, w_sem.at[1]),
        pltpu.make_async_copy(down_hbm.at[0], down_v, w_sem.at[2]),
    ]
    barrier = pltpu.get_barrier_semaphore()

    def greet(s, _):
        pl.semaphore_signal(barrier, inc=1, device_id=(lax.rem(me + s, n),), device_id_type=MESH)
        return 0

    lax.fori_loop(1, n, greet, 0)
    for copy in weights:
        copy.start()

    experts = lax.broadcasted_iota(jnp.int32, (n, tokens), 0)
    hot0 = (experts == ids_ref[0:1, :]).astype(F32)
    hot1 = (experts == ids_ref[1:2, :]).astype(F32)
    square = (tokens, tokens)
    before = (
        lax.broadcasted_iota(jnp.int32, square, 0) < lax.broadcasted_iota(jnp.int32, square, 1)
    ).astype(F32).astype(BF16)
    earlier0 = jnp.dot(hot0.astype(BF16), before, preferred_element_type=F32)
    earlier1 = jnp.dot(hot1.astype(BF16), before, preferred_element_type=F32)
    count0 = jnp.sum(hot0, axis=1, keepdims=True)
    stride = float(cap * parts)
    base0 = jnp.sum(hot0 * earlier0, axis=0, keepdims=True) + ids_ref[0:1, :].astype(F32) * stride
    base1 = (
        jnp.sum(hot1 * (earlier1 + count0), axis=0, keepdims=True)
        + ids_ref[1:2, :].astype(F32) * stride
    )

    total = jnp.zeros((tokens, 1), F32)
    for q in range(parts):
        wide = tok_ref[:, q * part:(q + 1) * part].astype(F32)
        total += jnp.sum(wide * wide, axis=1, keepdims=True)
    inverse = lax.rsqrt(total / width + 1e-05)
    for q in range(parts):
        cut = slice(q * part, (q + 1) * part)
        normed[:, cut] = (tok_ref[:, cut].astype(F32) * inverse * gain_ref[:, cut]).astype(BF16)

    pl.semaphore_wait(barrier, n - 1)

    def out_copy(h, j):
        return pltpu.make_async_remote_copy(
            src_ref=send.at[h, j], dst_ref=recv.at[h, place],
            send_sem=s1.at[h, j], recv_sem=r1.at[h, place],
            device_id=(block_of(h) * per + j,), device_id_type=MESH,
        )

    def in_copy(h, j):
        return pltpu.make_async_remote_copy(
            src_ref=send.at[h, j], dst_ref=recv.at[h, j],
            send_sem=s1.at[h, j], recv_sem=r1.at[h, j],
            device_id=(block_of(h) * per + j,), device_id_type=MESH,
        )

    def back_copy(h, j):
        return pltpu.make_async_remote_copy(
            src_ref=yout.at[h, j], dst_ref=ret.at[h, place],
            send_sem=s2.at[h, j], recv_sem=r2.at[h, place],
            device_id=(block_of(h) * per + j,), device_id_type=MESH,
        )

    def home_copy(h, j):
        return pltpu.make_async_remote_copy(
            src_ref=yout.at[h, j], dst_ref=ret.at[h, j],
            send_sem=s2.at[h, j], recv_sem=r2.at[h, j],
            device_id=(block_of(h) * per + j,), device_id_type=MESH,
        )

    def pick(order, i):
        return sum(jnp.where(i == k, h, 0) for k, h in enumerate(order))

    def each(h, act):
        def step(turn, _):
            j = lax.rem(place + turn, per)

            @pl.when(jnp.logical_or(h != 0, j != place))
            def _():
                act(j)
            return 0
        lax.fori_loop(0, per, step, 0)

    def dispatch(i, _):
        h = pick(SENT, i)
        first = (block_of(h) * rows).astype(F32)
        at = lax.broadcasted_iota(jnp.int32, (rows, tokens), 0).astype(F32) + first
        picked = jnp.zeros((rows, part), F32)
        for q in range(parts):
            shift = float(q * cap)
            hot = jnp.logical_or(at == base0 + shift, at == base1 + shift)
            picked += jnp.dot(
                hot.astype(F32).astype(BF16), normed[:, q * part:(q + 1) * part],
                preferred_element_type=F32,
            )
        send[h] = picked.astype(BF16).reshape(per, cap * parts, part)
        each(h, lambda j: out_copy(h, j).start())
        return 0

    lax.fori_loop(0, BLOCKS, dispatch, 0)
    recv[0, place] = send[0, place]

    logits = lax.dot_general(
        router_ref[...], normed[...], (((1,), (1,)), ((), ())), preferred_element_type=F32
    )
    first = jnp.sum(hot0 * logits, axis=0, keepdims=True)
    second = jnp.sum(hot1 * logits, axis=0, keepdims=True)
    weight0 = to_column(jax.nn.sigmoid(first - second))
    weight1 = to_column(jax.nn.sigmoid(second - first))
    column0, column1 = to_column(base0), to_column(base1)
    acc[...] = tok_ref[...].astype(F32)
    for copy in weights:
        copy.wait()

    def ffn(i, _):
        h = pick(WORKED, i)
        each(h, lambda j: in_copy(h, j).wait_recv())
        xs[...] = jnp.dot(
            split_ref[...], recv[h].reshape(rows, part), preferred_element_type=F32
        ).astype(BF16)
        hidden = gate_v.shape[1]
        gate = jnp.zeros((flat, hidden), F32)
        up = jnp.zeros((flat, hidden), F32)
        for q in range(parts):
            x = xs[q * flat:(q + 1) * flat, :]
            gate += jnp.dot(x, gate_v[q * part:(q + 1) * part, :], preferred_element_type=F32)
            up += jnp.dot(x, up_v[q * part:(q + 1) * part, :], preferred_element_type=F32)
        act = (gate / (1.0 + jnp.exp(-gate)) * up).astype(BF16)
        for q in range(parts):
            ys[q * flat:(q + 1) * flat, :] = jnp.dot(
                act, down_v[:, q * part:(q + 1) * part], preferred_element_type=F32
            ).astype(BF16)
        yout[h] = jnp.dot(
            merge_ref[...], ys[...], preferred_element_type=F32
        ).astype(BF16).reshape(per, cap * parts, part)
        each(h, lambda j: back_copy(h, j).start())
        return 0

    lax.fori_loop(0, BLOCKS, ffn, 0)
    ret[0, place] = yout[0, place]

    def combine(i, _):
        h = pick(TAKEN, i)
        each(h, lambda j: home_copy(h, j).wait_recv())
        start = (block_of(h) * rows).astype(F32)
        at = lax.broadcasted_iota(jnp.int32, (tokens, rows), 1).astype(F32) + start
        back = ret[h].reshape(rows, part)
        for q in range(parts):
            shift = float(q * cap)
            cut = slice(q * part, (q + 1) * part)
            hot_a = (at == column0 + shift).astype(F32).astype(BF16)
            hot_b = (at == column1 + shift).astype(F32).astype(BF16)
            acc[:, cut] += weight0 * jnp.dot(hot_a, back, preferred_element_type=F32)
            acc[:, cut] += weight1 * jnp.dot(hot_b, back, preferred_element_type=F32)
        return 0

    lax.fori_loop(0, BLOCKS, combine, 0)

    head = head_ref[...].astype(F32)
    lanes = head.shape[1]
    score = jnp.zeros((tokens, 1), F32)
    for q in range(parts):
        cut = slice(q * part, (q + 1) * part)
        mixed = acc[:, cut].astype(BF16)
        mixed_ref[:, cut] = mixed
        partial = jnp.zeros((tokens, lanes), F32)
        for k in range(part // lanes):
            row = q * (part // lanes) + k
            partial += mixed[:, k * lanes:(k + 1) * lanes].astype(F32) * head[row:row + 1, :]
        score += jnp.sum(partial, axis=1, keepdims=True)
    values = jnp.tanh(to_row(score))
    values_ref[...] = values
    error = values - target_ref[...].astype(F32)
    recency = recency_ref[...]
    weighted = jnp.sum(recency * error * error, axis=1, keepdims=True)
    weight = jnp.sum(recency, axis=1, keepdims=True)
    lane = lax.broadcasted_iota(jnp.int32, sums.shape, 1)
    sums[...] = jnp.where(lane == 0, weighted, jnp.where(lane == 1, weight, 0.0))
    all_sums[me] = sums[...]

    def sum_copy(to, slot):
        return pltpu.make_async_remote_copy(
            src_ref=sums, dst_ref=all_sums.at[slot],
            send_sem=s3.at[to], recv_sem=r3.at[slot],
            device_id=(to,), device_id_type=MESH,
        )

    def share(s, _):
        sum_copy(lax.rem(me + s, n), me).start()
        return 0

    lax.fori_loop(1, n, share, 0)

    def drain(h, _):
        each(h, lambda j: out_copy(h, j).wait_send())
        each(h, lambda j: back_copy(h, j).wait_send())
        return 0

    lax.fori_loop(0, BLOCKS, drain, 0)

    def take(s, _):
        other = lax.rem(me + s, n)
        sum_copy(other, other).wait_recv()
        return 0

    lax.fori_loop(1, n, take, 0)
    whole = jnp.sum(all_sums[...], axis=0)
    loss_ref[...] = whole[0:1, 0:1] / whole[0:1, 1:2]

    def leave(s, _):
        other = lax.rem(me + s, n)
        sum_copy(other, other).wait_send()
        return 0

    lax.fori_loop(1, n, leave, 0)


def body(
    axis,
    n,
    tokens,
    norm_gain,
    router_weight,
    expert_ids,
    gate_proj,
    up_proj,
    down_proj,
    value_weight,
    value_target,
    recency,
):
    count, width = tokens.shape
    hidden = gate_proj.shape[2]
    cap = 3 * count // n
    parts = 1
    while cap * parts % 16:
        parts *= 2
    part = width // parts
    per = n // BLOCKS
    rows, flat = per * cap * parts, per * cap
    order = np.arange(rows).reshape(per, parts, cap).transpose(1, 0, 2).reshape(-1)
    split = np.zeros((rows, rows), np.float32)
    split[np.arange(rows), order] = 1.0
    merge = jnp.asarray(split.T, BF16)
    split = jnp.asarray(split, BF16)
    vmem = pl.BlockSpec(memory_space=pltpu.VMEM)
    block = (BLOCKS, per, cap * parts, part)
    dma = pltpu.SemaphoreType.DMA
    mixed, values, loss = pl.pallas_call(
        functools.partial(kernel, axis, n, cap, parts),
        out_shape=(
            jax.ShapeDtypeStruct((count, width), BF16),
            jax.ShapeDtypeStruct((1, count), F32),
            jax.ShapeDtypeStruct((1, 1), F32),
        ),
        in_specs=[vmem] * 9 + [pl.BlockSpec(memory_space=pl.ANY)] * 3,
        out_specs=(vmem, vmem, vmem),
        scratch_shapes=[
            pltpu.VMEM((width, hidden), BF16),
            pltpu.VMEM((width, hidden), BF16),
            pltpu.VMEM((hidden, width), BF16),
            pltpu.VMEM((count, width), BF16),
            pltpu.VMEM(block, BF16),
            pltpu.VMEM(block, BF16),
            pltpu.VMEM((rows, part), BF16),
            pltpu.VMEM((rows, part), BF16),
            pltpu.VMEM(block, BF16),
            pltpu.VMEM(block, BF16),
            pltpu.VMEM((count, width), F32),
            pltpu.VMEM((8, 128), F32),
            pltpu.VMEM((n, 8, 128), F32),
            dma((3,)),
            dma((BLOCKS, per)),
            dma((BLOCKS, per)),
            dma((BLOCKS, per)),
            dma((BLOCKS, per)),
            dma((n,)),
            dma((n,)),
        ],
        compiler_params=pltpu.CompilerParams(
            collective_id=0, has_side_effects=True, vmem_limit_bytes=60 * 2**20
        ),
        cost_estimate=pl.CostEstimate(
            flops=6 * n * cap * width * hidden,
            bytes_accessed=6 * width * hidden,
            transcendentals=n * cap * hidden,
        ),
    )(
        tokens,
        norm_gain.reshape(1, width),
        router_weight.T,
        expert_ids.T,
        value_weight.reshape(width // 128, 128),
        value_target.reshape(1, count),
        recency.reshape(1, count),
        split,
        merge,
        gate_proj,
        up_proj,
        down_proj,
    )
    return (mixed, values.reshape(count), loss.reshape(()))


def solution(mesh):
    axis = mesh.axis_names[0]
    return jax.shard_map(
        functools.partial(body, axis, mesh.shape[axis]),
        mesh=mesh,
        in_specs=(
            P(axis, None),
            P(),
            P(),
            P(axis, None),
            P(axis, None, None),
            P(axis, None, None),
            P(axis, None, None),
            P(),
            P(axis),
            P(axis),
        ),
        out_specs=(P(axis, None), P(axis), P()),
        check_vma=False,
    )
```
